32 devices in a mesh: dp: 4 (over y, x), context: 8 (over z, core).
Axes of the slice: x: 2, y: 2, z: 4, core: 2. Of those that a mesh axis runs over, the one named last changes fastest.
Arguments:
- queries: bfloat16 [4, 1024, 2048], P('dp', 'context'), may hold values from -6 to 6
- keys: bfloat16 [4, 1024, 2048], P('dp', 'context'), may hold values from -6 to 6
- values: bfloat16 [4, 1024, 2048], P('dp', 'context'), may hold values from -40 to 40
- gain: float32 [2048], replicated, may hold values from 0.1 to 1.9
- out_grad: bfloat16 [4, 1024, 2048], P('dp', 'context'), may hold values from -6 to 6
Outputs:
- query_grad: bfloat16 [4, 1024, 2048], P('dp', 'context')
- key_grad: bfloat16 [4, 1024, 2048], P('dp', 'context')
- value_grad: bfloat16 [4, 1024, 2048], P('dp', 'context')
- scale_factor_sensitivity: float32 [2048], replicated
The draws below stay inside these ranges and needn't reach their ends.
All inputs are finite; a program needn't handle non-finite values.
Results may differ from the reference program's by a relative error of at most 0.0067.
Values may be sent and summed in bfloat16 or wider, within the bound.
A program may use at most 64 MiB of HBM per device.

```python
import math
import jax
import jax.numpy as jnp
from jax import lax

HEADS = 16
HEAD_DIM = 128
TOK_DEV = 128
FEATURES = 2048
LENGTH = 1024
SEQS = 4
N_CONTEXT = 8


def draw_values(key, part):
    key = jax.random.fold_in(key, 11)
    first, second = jax.random.split(key, 2)
    columns = jnp.exp(jax.random.uniform(first, (HEADS * HEAD_DIM,), jnp.float32, 0.0, math.log(10.0)))
    shape = (SEQS, LENGTH, HEADS * HEAD_DIM)
    raw = jnp.clip(jax.random.normal(second, shape, jnp.float32), -4.0, 4.0)
    return (raw * columns).astype(jnp.bfloat16)


def draw_out_grad(key, part):
    key = jax.random.fold_in(key, 23)
    shape = (SEQS, LENGTH, HEADS * HEAD_DIM)
    place = ((jnp.arange(LENGTH, dtype=jnp.float32) + 0.5) / LENGTH)[None, :, None]
    raw = jnp.clip(jax.random.normal(key, shape, jnp.float32), -4.0, 4.0) * (0.5 + place)
    return raw.astype(jnp.bfloat16)


def level_of(key, dims, pieces, least, top_value):
    level, own = 1.0, jax.random.fold_in(key, 6)
    for dim, blocks in pieces:
        draws = jnp.exp(jax.random.uniform(jax.random.fold_in(own, dim), (blocks,), jnp.float32, least / len(pieces), top_value / len(pieces)))
        level = level * jnp.repeat(draws, dims[dim] // blocks).reshape([-1 if axis == dim else 1 for axis in range(len(dims))])
    return level


def noise(own_key, dims, width, bound, cuts=(), kind=jnp.bfloat16):
    entries = jax.random.normal(own_key, dims, jnp.float32) * width
    if len(cuts) > 0:
        entries = level_of(own_key, dims, cuts, -0.22, 0.18) * entries
    return jnp.clip(entries, min=-bound, max=bound).astype(kind)


def setup_inputs(seed: int = 0) -> dict:
    streams_of = jax.random.split(jax.random.key(seed), 6)
    return {
        "queries": noise(streams_of[0], (SEQS, LENGTH, FEATURES), 1.0, 6.0, ((0, 4), (1, 8))),
        "keys": noise(streams_of[1], (SEQS, LENGTH, FEATURES), 1.0, 6.0, ((0, 4), (1, 8))),
        "values": draw_values(jax.random.fold_in(streams_of[5], 71), 0),
        "gain": jnp.clip(1.0 + 0.18 * jax.random.normal(streams_of[3], (FEATURES,), jnp.float32), 0.1, 1.9),
        "out_grad": draw_out_grad(jax.random.fold_in(streams_of[5], 71), 0),
    }


def blocks_of(array):
    shaped = array.reshape(N_CONTEXT, TOK_DEV, HEADS, HEAD_DIM)
    return jnp.transpose(shaped, (0, 2, 1, 3)).astype(jnp.float32)

def unblock(array):
    return jnp.transpose(array, (0, 2, 1, 3)).reshape(LENGTH, HEADS * HEAD_DIM).astype(jnp.bfloat16)

def one_sequence(items, gain):
    probe_vectors, key_matrix, payload_table, grad_rows = items
    qf = blocks_of(probe_vectors)
    kf = blocks_of(key_matrix)
    vf = blocks_of(payload_table)
    dyf = blocks_of(grad_rows)
    within_block_part = jnp.einsum('bhck,bhcv->bhkv', kf, vf)
    zeros = jnp.zeros((1, HEADS, HEAD_DIM, HEAD_DIM), jnp.float32)
    leading_span = jnp.concatenate([zeros, jnp.cumsum(within_block_part, axis=0)[:-1]], axis=0)
    earlier_memory_tile = leading_span.astype(jnp.bfloat16).astype(jnp.float32)
    rows = jnp.arange(TOK_DEV, dtype=jnp.int32)
    causal = rows[:, None] >= rows[None, :]
    scores = jnp.einsum('bhck,bhsk->bhcs', qf, kf)
    attn = jnp.where(causal, scores, 0.0).astype(jnp.bfloat16).astype(jnp.float32)
    unnormed_output = jnp.einsum('bhck,bhkv->bhcv', qf, earlier_memory_tile) + jnp.einsum('bhcs,bhsv->bhcv', attn, vf)
    rms = jnp.sqrt(lax.optimization_barrier(jnp.mean(unnormed_output * unnormed_output, axis=-1, keepdims=True)) + 1e-06)
    unit = unnormed_output / rms
    scale = gain.reshape(HEADS, HEAD_DIM)[None, :, None, :]
    gain_part = lax.optimization_barrier(jnp.sum(dyf * unit, axis=(0, 2)))
    scaled = scale * dyf
    du = (scaled - unit * lax.optimization_barrier(jnp.mean(scaled * unit, axis=-1, keepdims=True))) / rms
    normed_output_grad = du.astype(jnp.bfloat16).astype(jnp.float32)
    addend_piece = jnp.einsum('bhck,bhcv->bhkv', qf, normed_output_grad)
    after = jnp.flip(jnp.cumsum(jnp.flip(addend_piece, 0), axis=0), 0)
    suffix = jnp.concatenate([after[1:], zeros], axis=0)
    suffix_state_block = suffix.astype(jnp.bfloat16).astype(jnp.float32)
    dscores = jnp.einsum('bhcv,bhsv->bhcs', normed_output_grad, vf)
    dattn = jnp.where(causal, dscores, 0.0).astype(jnp.bfloat16).astype(jnp.float32)
    probe_sensitivity = jnp.einsum('bhcv,bhkv->bhck', normed_output_grad, earlier_memory_tile) + jnp.einsum('bhcs,bhsk->bhck', dattn, kf)
    key_derivative = jnp.einsum('bhcs,bhck->bhsk', dattn, qf) + jnp.einsum('bhsv,bhkv->bhsk', vf, suffix_state_block)
    payload_sensitivity = jnp.einsum('bhcs,bhcv->bhsv', attn, normed_output_grad) + jnp.einsum('bhsk,bhkv->bhsv', kf, suffix_state_block)
    return (unblock(probe_sensitivity), unblock(key_derivative), unblock(payload_sensitivity), gain_part)

def reference(queries, keys, values, gain, out_grad):
    probe_sensitivity, key_derivative, payload_sensitivity, parts = lax.map(lambda items: one_sequence(items, gain), (queries, keys, values, out_grad))
    total = lax.optimization_barrier(jnp.sum(parts, axis=0)).reshape(HEADS * HEAD_DIM)
    scale_factor_sensitivity = total / jnp.sqrt(jnp.float32(SEQS * LENGTH))
    return (probe_sensitivity, key_derivative, payload_sensitivity, scale_factor_sensitivity)
```

```python
import functools
import math

import jax
import jax.numpy as jnp
from jax import lax
from jax.experimental import pallas as pl
from jax.experimental.pallas import tpu as pltpu
from jax.sharding import PartitionSpec as P

HEADS = 16
HALF = HEADS // 2
DIM = 128
F32 = jnp.float32
BF16 = jnp.bfloat16
MESH = pl.DeviceIdType.MESH


def nn(a, b):
    return lax.dot_general(a, b, (((1,), (0,)), ((), ())), preferred_element_type=F32)


def nt(a, b):
    return lax.dot_general(a, b, (((1,), (1,)), ((), ())), preferred_element_type=F32)


def tn(a, b):
    return lax.dot_general(a, b, (((0,), (0,)), ((), ())), preferred_element_type=F32)


def kernel(
    n_dp, n_ctx, tokens, link_t,
    q_ref, k_ref, v_ref, gain_ref, dy_ref,
    qg_ref, kg_ref, vg_ref, sg_ref,
    loc, xs, xr, ps, pr, fs, pre, attn, du, term, ts, tr, rs, rr, ss, suf, kp, vp,
    gloc, g1, g2, gout,
    x_sem, p_sem, f_sem, t_sem, r_sem, s_sem, g1s, g1r, g2s, g2r, g3s, g3r,
):
    dp = lax.axis_index("dp")
    ctx = lax.axis_index("context")
    chips = n_ctx // 2
    last = chips - 1
    z = ctx // 2
    core = ctx % 2
    sib = z * 2 + (1 - core)
    own0 = core * HALF
    sib0 = (1 - core) * HALF
    per = gout.shape[1]
    n_own = gout.shape[0]

    barrier = pltpu.get_barrier_semaphore()

    @pl.loop(0, n_ctx)
    def _(c):
        @pl.when(c != ctx)
        def _():
            pl.semaphore_signal(barrier, inc=1, device_id={"context": c}, device_id_type=MESH)

    @pl.loop(0, n_dp)
    def _(d):
        @pl.when(d != dp)
        def _():
            pl.semaphore_signal(barrier, inc=1, device_id={"dp": d}, device_id_type=MESH)

    def lanes(h):
        return pl.ds(pl.multiple_of(h * DIM, DIM), DIM)

    def remote(src, dst, sems, i, device):
        return pltpu.make_async_remote_copy(
            src_ref=src, dst_ref=dst, send_sem=sems.at[0, i], recv_sem=sems.at[1, i],
            device_id={"context": device}, device_id_type=MESH,
        )

    def swap_local(t):
        return remote(xs.at[t], xr.at[t], x_sem, t, sib)

    def pass_prefix(t):
        return remote(ps.at[t], pr.at[t], p_sem, t, jnp.minimum(ctx + 2, n_ctx - 2 + core))

    def give_prefix(t):
        return remote(fs.at[t], pre.at[own0 + t], f_sem, t, sib)

    def swap_term(t):
        return remote(ts.at[t], tr.at[t], t_sem, t, sib)

    def pass_suffix(t):
        return remote(rs.at[t], rr.at[t], r_sem, t, jnp.maximum(ctx - 2, core))

    def give_suffix(t):
        return remote(ss.at[t], suf.at[own0 + t], s_sem, t, sib)

    @pl.loop(0, HALF // 2)
    def _(i):
        for j in range(2):
            t = i * 2 + j
            s = lanes(sib0 + t)
            xs[t] = tn(k_ref[:, s], v_ref[:, s]).astype(BF16)

    pl.semaphore_wait(barrier, n_ctx - 1 + n_dp - 1)

    @pl.loop(0, HALF)
    def _(t):
        swap_local(t).start()

    @pl.loop(0, HALF // 2)
    def _(i):
        for j in range(2):
            t = i * 2 + j
            s = lanes(own0 + t)
            loc[t] = tn(k_ref[:, s], v_ref[:, s])

    @pl.when(z == 0)
    def _():
        pr[...] = jnp.zeros_like(pr)

    @pl.when(z == last)
    def _():
        rr[...] = jnp.zeros_like(rr)

    def prefix_chain(t):
        swap_local(t).wait_recv()

        @pl.when(z > 0)
        def _():
            pass_prefix(t).wait_recv()

        before = pr[t].astype(F32)
        other = xr[t].astype(F32)
        mine = loc[t]

        @pl.when(z < last)
        def _():
            ps[t] = (before + (mine + other)).astype(link_t)
            pass_prefix(t).start()

        @pl.when(core == 0)
        def _():
            fs[t] = (before + mine).astype(BF16)
            give_prefix(t).start()
            pre[own0 + t] = before.astype(BF16)

        @pl.when(core == 1)
        def _():
            fs[t] = before.astype(BF16)
            give_prefix(t).start()
            pre[own0 + t] = (before + other).astype(BF16)

    @pl.when(z == 0)
    def _():
        @pl.loop(0, HALF)
        def _(t):
            prefix_chain(t)

    rows = lax.broadcasted_iota(jnp.int32, (DIM, DIM), 0)
    cols = lax.broadcasted_iota(jnp.int32, (DIM, DIM), 1)

    @pl.loop(0, HEADS // 4)
    def _(i):
        for j in range(4):
            h = i * 4 + j
            s = lanes(h)
            attn[h] = jnp.where(rows >= cols, nt(q_ref[:, s], k_ref[:, s]), 0.0).astype(BF16)

    def through_norm(h):
        s = lanes(h)
        u = nn(q_ref[:, s], pre[h]) + nn(attn[h], v_ref[:, s])
        inv = lax.rsqrt(jnp.mean(u * u, axis=-1, keepdims=True) + 1e-6)
        unit = u * inv
        grad = dy_ref[:, s].astype(F32)
        gloc[h] = jnp.sum(grad * unit, axis=0, keepdims=True)
        scaled = gain_ref[:, s] * grad
        d = (scaled - unit * jnp.mean(scaled * unit, axis=-1, keepdims=True)) * inv
        d = d.astype(BF16)
        du[h] = d
        return tn(q_ref[:, s], d)

    def norm_step(t):
        remote(fs.at[t], pre.at[sib0 + t], f_sem, t, sib).wait_recv()
        other = through_norm(sib0 + t)
        mine = through_norm(own0 + t)
        ts[t] = other.astype(BF16)
        swap_term(t).start()
        term[t] = mine

    def suffix_chain(t):
        swap_term(t).wait_recv()

        @pl.when(z < last)
        def _():
            pass_suffix(t).wait_recv()

        after = rr[t].astype(F32)
        other = tr[t].astype(F32)
        mine = term[t]

        @pl.when(z > 0)
        def _():
            rs[t] = (after + (mine + other)).astype(link_t)
            pass_suffix(t).start()

        @pl.when(core == 0)
        def _():
            ss[t] = after.astype(BF16)
            give_suffix(t).start()
            suf[own0 + t] = (after + other).astype(BF16)

        @pl.when(core == 1)
        def _():
            ss[t] = (after + mine).astype(BF16)
            give_suffix(t).start()
            suf[own0 + t] = after.astype(BF16)

    def within_block(h):
        s = lanes(h)
        d = du[h]
        da = jnp.where(rows >= cols, nt(d, v_ref[:, s]), 0.0).astype(BF16)
        qg_ref[:, s] = (nt(d, pre[h]) + nn(da, k_ref[:, s])).astype(BF16)
        kp[h] = tn(da, q_ref[:, s])
        vp[h] = tn(attn[h], d)

    def finish(h):
        s = lanes(h)
        kg_ref[:, s] = (kp[h] + nt(v_ref[:, s], suf[h])).astype(BF16)
        vg_ref[:, s] = (vp[h] + nn(k_ref[:, s], suf[h])).astype(BF16)

    def gain_copy(src, dst, send, recv, device):
        return pltpu.make_async_remote_copy(
            src_ref=src, dst_ref=dst, send_sem=send, recv_sem=recv,
            device_id=device, device_id_type=MESH,
        )

    def to_owner(o):
        return gain_copy(
            gloc.at[pl.ds(o * per, per)], g1.at[ctx], g1s.at[o], g1r.at[ctx], {"context": o})

    def across(d):
        return gain_copy(g2.at[dp], g2.at[dp], g2s.at[d], g2r.at[dp], {"dp": d})

    def to_all(c):
        return gain_copy(gout.at[ctx], gout.at[ctx], g3s.at[c], g3r.at[ctx], {"context": c})

    def others(n, me, f):
        @pl.loop(0, n)
        def _(i):
            @pl.when(i != me)
            def _():
                f(i)

    def gain_first():
        others(n_own, ctx, lambda o: to_owner(o).start())

        @pl.when(ctx < n_own)
        def _():
            g1[ctx] = gloc[pl.ds(ctx * per, per)]

    def gain_second():
        @pl.when(ctx < n_own)
        def _():
            others(n_ctx, ctx, lambda c: gain_copy(
                gloc.at[pl.ds(0, per)], g1.at[c], g1s.at[0], g1r.at[c], {"context": c}).wait_recv())
            g2[dp] = jnp.sum(g1[...], axis=0)
            others(n_dp, dp, lambda d: across(d).start())

    def gain_third():
        @pl.when(ctx < n_own)
        def _():
            others(n_dp, dp, lambda d: gain_copy(
                g2.at[d], g2.at[d], g2s.at[d], g2r.at[d], {"dp": d}).wait_recv())
            gout[ctx] = jnp.sum(g2[...], axis=0) / jnp.sqrt(F32(tokens))
            others(n_ctx, ctx, lambda c: to_all(c).start())

    chain_lag = jnp.minimum(2 + HALF * (last - z), 2 * HALF + 1)
    finish_lag = jnp.maximum(chain_lag, HALF + 1) + 1

    @pl.loop(0, 3 * HALF + 2)
    def _(t):
        @pl.when((t < HALF) & (z > 0))
        def _():
            prefix_chain(t)

        @pl.when((t >= 1) & (t < HALF + 1))
        def _():
            norm_step(t - 1)

        @pl.when(t == HALF)
        def _():
            gain_first()

        c = t - chain_lag

        @pl.when((c >= 0) & (c < HALF))
        def _():
            suffix_chain(c)

        @pl.when(c == HALF - 1)
        def _():
            gain_second()

        w = t - (HALF + 1)

        @pl.when((w >= 0) & (w < HALF))
        def _():
            within_block(own0 + w)
            within_block(sib0 + w)

        f = t - finish_lag

        @pl.when((f >= 0) & (f < HALF))
        def _():
            remote(ss.at[f], suf.at[sib0 + f], s_sem, f, sib).wait_recv()
            finish(own0 + f)
            finish(sib0 + f)

    gain_third()
    others(n_own, ctx, lambda o: gain_copy(
        gout.at[o], gout.at[o], g3s.at[o], g3r.at[o], {"context": o}).wait_recv())
    for h in range(HEADS):
        sg_ref[:, h * DIM:(h + 1) * DIM] = gout[h // per, h % per]

    @pl.loop(0, HALF)
    def _(t):
        swap_local(t).wait_send()
        give_prefix(t).wait_send()
        swap_term(t).wait_send()
        give_suffix(t).wait_send()

        @pl.when(z < last)
        def _():
            pass_prefix(t).wait_send()

        @pl.when(z > 0)
        def _():
            pass_suffix(t).wait_send()

    others(n_own, ctx, lambda o: to_owner(o).wait_send())

    @pl.when(ctx < n_own)
    def _():
        others(n_dp, dp, lambda d: across(d).wait_send())
        others(n_ctx, ctx, lambda c: to_all(c).wait_send())


def shards(n_dp, n_ctx, queries, keys, values, gain, out_grad):
    count, width = queries.shape[1:]
    tokens = queries.shape[0] * n_dp * count * n_ctx
    link_t = BF16 if n_ctx <= 16 else F32
    n_own = min(n_ctx, HEADS)
    per = HEADS // n_own
    flat = lambda x: x.reshape(count, width)
    tile = lambda n, t: pltpu.VMEM((n, DIM, DIM), t)
    vmem = pl.BlockSpec(memory_space=pltpu.VMEM)
    dma = pltpu.SemaphoreType.DMA
    outs = pl.pallas_call(
        functools.partial(kernel, n_dp, n_ctx, tokens, link_t),
        out_shape=[jax.ShapeDtypeStruct((count, width), BF16)] * 3
        + [jax.ShapeDtypeStruct((1, width), F32)],
        in_specs=[vmem] * 5,
        out_specs=[vmem] * 4,
        scratch_shapes=[
            tile(HALF, F32), tile(HALF, BF16), tile(HALF, BF16),
            tile(HALF, link_t), tile(HALF, link_t), tile(HALF, BF16), tile(HEADS, BF16),
            tile(HEADS, BF16), tile(HEADS, BF16),
            tile(HALF, F32), tile(HALF, BF16), tile(HALF, BF16),
            tile(HALF, link_t), tile(HALF, link_t), tile(HALF, BF16), tile(HEADS, BF16),
            tile(HEADS, F32), tile(HEADS, F32),
            pltpu.VMEM((HEADS, 1, DIM), F32),
            pltpu.VMEM((n_ctx, per, 1, DIM), F32),
            pltpu.VMEM((n_dp, per, 1, DIM), F32),
            pltpu.VMEM((n_own, per, 1, DIM), F32),
        ]
        + [dma((2, HALF))] * 6
        + [dma((n_own,)), dma((n_ctx,)), dma((n_dp,)), dma((n_dp,)), dma((n_ctx,)), dma((n_own,))],
        compiler_params=pltpu.CompilerParams(
            collective_id=0, has_side_effects=True, vmem_limit_bytes=40 * 2**20),
        cost_estimate=pl.CostEstimate(
            flops=24 * HEADS * DIM**3, bytes_accessed=7 * 2 * count * width,
            transcendentals=HEADS * DIM),
    )(flat(queries), flat(keys), flat(values), gain.reshape(1, width), flat(out_grad))
    shape = (1, count, width)
    return (outs[0].reshape(shape), outs[1].reshape(shape), outs[2].reshape(shape),
            outs[3].reshape(width))


def solution(mesh):
    rows = P("dp", "context", None)
    return jax.shard_map(
        functools.partial(shards, mesh.shape["dp"], mesh.shape["context"]),
        mesh=mesh,
        in_specs=(rows, rows, rows, P(), rows),
        out_specs=(rows, rows, rows, P()),
        check_vma=False,
    )
```

```python
import functools
import math

import jax
import jax.numpy as jnp
from jax import lax
from jax.experimental import pallas as pl
from jax.experimental.pallas import tpu as pltpu
from jax.sharding import PartitionSpec as P

HEADS = 16
HALF = HEADS // 2
WIDE = 1
PARTS = HALF // WIDE
NORM_LAG = 1
CHAIN_LAG = 1
FINISH_LAG = 1
DIM = 128
F32 = jnp.float32
BF16 = jnp.bfloat16
MESH = pl.DeviceIdType.MESH


def nn(a, b):
    return lax.dot_general(a, b, (((1,), (0,)), ((), ())), preferred_element_type=F32)


def nt(a, b):
    return lax.dot_general(a, b, (((1,), (1,)), ((), ())), preferred_element_type=F32)


def tn(a, b):
    return lax.dot_general(a, b, (((0,), (0,)), ((), ())), preferred_element_type=F32)


def kernel(
    n_dp, n_ctx, tokens, link_t,
    q_hbm, k_hbm, v_hbm, gain_hbm, dy_hbm,
    qg_hbm, kg_hbm, vg_hbm, sg_hbm,
    q_ref, k_ref, v_ref, gain_ref, dy_ref, qg_ref, kg_ref, vg_ref, sg_ref,
    loc, xs, xr, ps, pr, fs, pre, attn, du, term, ts, tr, rs, rr, ss, suf, kp, vp,
    gloc, g1, g2, gout,
    x_sem, p_sem, f_sem, t_sem, r_sem, s_sem, g1s, g1r, g2s, g2r, g3s, g3r, in_sem, out_sem,
):
    dp = lax.axis_index("dp")
    ctx = lax.axis_index("context")
    chips = n_ctx // 2
    last = chips - 1
    z = ctx // 2
    core = ctx % 2
    sib = z * 2 + (1 - core)
    own0 = core * HALF
    sib0 = (1 - core) * HALF
    per = gout.shape[1]
    n_own = gout.shape[0]

    def lanes(h):
        return pl.ds(pl.multiple_of(h * DIM, DIM), DIM)

    def half(h):
        return pl.ds(pl.multiple_of(h * DIM, DIM), HALF * DIM)

    sh, oh = half(sib0), half(own0)
    loads = [
        pltpu.make_async_copy(src, dst, in_sem.at[i])
        for i, (src, dst) in enumerate([
            (k_hbm.at[:, sh], k_ref.at[:, sh]), (v_hbm.at[:, sh], v_ref.at[:, sh]),
            (k_hbm.at[:, oh], k_ref.at[:, oh]), (v_hbm.at[:, oh], v_ref.at[:, oh]),
            (q_hbm, q_ref), (dy_hbm, dy_ref), (gain_hbm, gain_ref)])
    ]
    for load in loads:
        load.start()

    barrier = pltpu.get_barrier_semaphore()

    @pl.loop(0, n_ctx)
    def _(c):
        @pl.when(c != ctx)
        def _():
            pl.semaphore_signal(barrier, inc=1, device_id={"context": c}, device_id_type=MESH)

    @pl.loop(0, n_dp)
    def _(d):
        @pl.when(d != dp)
        def _():
            pl.semaphore_signal(barrier, inc=1, device_id={"dp": d}, device_id_type=MESH)

    def part(t, base=0):
        return pl.ds(base + t * WIDE, WIDE)

    def remote(src, dst, sems, i, device):
        return pltpu.make_async_remote_copy(
            src_ref=src, dst_ref=dst, send_sem=sems.at[0, i], recv_sem=sems.at[1, i],
            device_id={"context": device}, device_id_type=MESH,
        )

    def swap_local(t):
        return remote(xs.at[part(t)], xr.at[part(t)], x_sem, t, sib)

    def pass_prefix(t):
        return remote(ps.at[part(t)], pr.at[part(t)], p_sem, t, jnp.minimum(ctx + 2, n_ctx - 2 + core))

    def give_prefix(t):
        return remote(fs.at[part(t)], pre.at[part(t, own0)], f_sem, t, sib)

    def swap_term(t):
        return remote(ts.at[part(t)], tr.at[part(t)], t_sem, t, sib)

    def pass_suffix(t):
        return remote(rs.at[part(t)], rr.at[part(t)], r_sem, t, jnp.maximum(ctx - 2, core))

    def give_suffix(t):
        return remote(ss.at[part(t)], suf.at[part(t, own0)], s_sem, t, sib)

    loads[0].wait()
    loads[1].wait()

    @pl.loop(0, HALF // 4)
    def _(i):
        for j in range(4):
            t = i * 4 + j
            s = lanes(sib0 + t)
            xs[t] = tn(k_ref[:, s], v_ref[:, s]).astype(BF16)

    pl.semaphore_wait(barrier, n_ctx - 1 + n_dp - 1)

    @pl.loop(0, PARTS)
    def _(t):
        swap_local(t).start()

    loads[2].wait()
    loads[3].wait()

    @pl.loop(0, HALF // 4)
    def _(i):
        for j in range(4):
            t = i * 4 + j
            s = lanes(own0 + t)
            loc[t] = tn(k_ref[:, s], v_ref[:, s])

    @pl.when(z == 0)
    def _():
        pr[...] = jnp.zeros_like(pr)

    @pl.when(z == last)
    def _():
        rr[...] = jnp.zeros_like(rr)

    def prefix_chain(t):
        swap_local(t).wait_recv()

        @pl.when(z > 0)
        def _():
            pass_prefix(t).wait_recv()

        before = pr[part(t)].astype(F32)
        other = xr[part(t)].astype(F32)
        mine = loc[part(t)]

        @pl.when(z < last)
        def _():
            ps[part(t)] = (before + (mine + other)).astype(link_t)
            pass_prefix(t).start()

        @pl.when(core == 0)
        def _():
            fs[part(t)] = (before + mine).astype(BF16)
            give_prefix(t).start()
            pre[part(t, own0)] = before.astype(BF16)

        @pl.when(core == 1)
        def _():
            fs[part(t)] = before.astype(BF16)
            give_prefix(t).start()
            pre[part(t, own0)] = (before + other).astype(BF16)

    @pl.when(z == 0)
    def _():
        @pl.loop(0, PARTS)
        def _(t):
            prefix_chain(t)

    for load in loads[4:]:
        load.wait()

    rows = lax.broadcasted_iota(jnp.int32, (DIM, DIM), 0)
    cols = lax.broadcasted_iota(jnp.int32, (DIM, DIM), 1)

    @pl.loop(0, HEADS // 4)
    def _(i):
        for j in range(4):
            h = i * 4 + j
            s = lanes(h)
            attn[h] = jnp.where(rows >= cols, nt(q_ref[:, s], k_ref[:, s]), 0.0).astype(BF16)

    def through_norm(h):
        s = lanes(h)
        u = nn(q_ref[:, s], pre[h]) + nn(attn[h], v_ref[:, s])
        inv = lax.rsqrt(jnp.mean(u * u, axis=-1, keepdims=True) + 1e-6)
        unit = u * inv
        grad = dy_ref[:, s].astype(F32)
        gloc[h] = jnp.sum(grad * unit, axis=0, keepdims=True)
        scaled = gain_ref[:, s] * grad
        d = (scaled - unit * jnp.mean(scaled * unit, axis=-1, keepdims=True)) * inv
        d = d.astype(BF16)
        du[h] = d
        return tn(q_ref[:, s], d)

    def norm_step(t):
        remote(fs.at[part(t)], pre.at[part(t, sib0)], f_sem, t, sib).wait_recv()
        other = through_norm(sib0 + t)
        mine = through_norm(own0 + t)
        ts[t] = other.astype(BF16)
        swap_term(t).start()
        term[t] = mine

    def suffix_chain(t):
        swap_term(t).wait_recv()

        @pl.when(z < last)
        def _():
            pass_suffix(t).wait_recv()

        after = rr[part(t)].astype(F32)
        other = tr[part(t)].astype(F32)
        mine = term[part(t)]

        @pl.when(z > 0)
        def _():
            rs[part(t)] = (after + (mine + other)).astype(link_t)
            pass_suffix(t).start()

        @pl.when(core == 0)
        def _():
            ss[part(t)] = after.astype(BF16)
            give_suffix(t).start()
            suf[part(t, own0)] = (after + other).astype(BF16)

        @pl.when(core == 1)
        def _():
            ss[part(t)] = (after + mine).astype(BF16)
            give_suffix(t).start()
            suf[part(t, own0)] = after.astype(BF16)

    def store(i, h):
        src, dst = ((qg_ref, qg_hbm), (kg_ref, kg_hbm), (vg_ref, vg_hbm))[i]
        s = lanes(h)
        return pltpu.make_async_copy(src.at[:, s], dst.at[:, s], out_sem.at[i, h])

    def within_block(h):
        s = lanes(h)
        d = du[h]
        da = jnp.where(rows >= cols, nt(d, v_ref[:, s]), 0.0).astype(BF16)
        qg_ref[:, s] = (nt(d, pre[h]) + nn(da, k_ref[:, s])).astype(BF16)
        kp[h] = tn(da, q_ref[:, s])
        vp[h] = tn(attn[h], d)

    def finish(h):
        s = lanes(h)
        kg_ref[:, s] = (kp[h] + nt(v_ref[:, s], suf[h])).astype(BF16)
        vg_ref[:, s] = (vp[h] + nn(k_ref[:, s], suf[h])).astype(BF16)

    def gain_copy(src, dst, send, recv, device):
        return pltpu.make_async_remote_copy(
            src_ref=src, dst_ref=dst, send_sem=send, recv_sem=recv,
            device_id=device, device_id_type=MESH,
        )

    def to_owner(o):
        return gain_copy(
            gloc.at[pl.ds(o * per, per)], g1.at[ctx], g1s.at[o], g1r.at[ctx], {"context": o})

    def across(d):
        return gain_copy(g2.at[dp], g2.at[dp], g2s.at[d], g2r.at[dp], {"dp": d})

    def to_all(c):
        return gain_copy(gout.at[ctx], gout.at[ctx], g3s.at[c], g3r.at[ctx], {"context": c})

    def others(n, me, f):
        @pl.loop(0, n)
        def _(i):
            @pl.when(i != me)
            def _():
                f(i)

    def gain_first():
        others(n_own, ctx, lambda o: to_owner(o).start())

        @pl.when(ctx < n_own)
        def _():
            g1[ctx] = gloc[pl.ds(ctx * per, per)]

    def gain_second():
        @pl.when(ctx < n_own)
        def _():
            others(n_ctx, ctx, lambda c: gain_copy(
                gloc.at[pl.ds(0, per)], g1.at[c], g1s.at[0], g1r.at[c], {"context": c}).wait_recv())
            g2[dp] = jnp.sum(g1[...], axis=0)
            others(n_dp, dp, lambda d: across(d).start())

    def gain_third():
        @pl.when(ctx < n_own)
        def _():
            others(n_dp, dp, lambda d: gain_copy(
                g2.at[d], g2.at[d], g2s.at[d], g2r.at[d], {"dp": d}).wait_recv())
            gout[ctx] = jnp.sum(g2[...], axis=0) / jnp.sqrt(F32(tokens))
            others(n_ctx, ctx, lambda c: to_all(c).start())

    chain_lag = jnp.minimum(
        NORM_LAG + CHAIN_LAG + PARTS * (last - z), 2 * PARTS + NORM_LAG)
    within_lag = PARTS + NORM_LAG
    finish_lag = jnp.maximum(chain_lag, within_lag) + FINISH_LAG

    gain_step = chain_lag + PARTS - 1 - jnp.clip(last - z - 1, 0, 2)

    @pl.loop(0, 3 * PARTS + NORM_LAG + CHAIN_LAG + FINISH_LAG)
    def _(t):
        @pl.when((t < PARTS) & (z > 0))
        def _():
            prefix_chain(t)

        @pl.when((t >= NORM_LAG) & (t < PARTS + NORM_LAG))
        def _():
            norm_step(t - NORM_LAG)

        @pl.when(t == PARTS - 1 + NORM_LAG)
        def _():
            gain_first()

        c = t - chain_lag

        @pl.when((c >= 0) & (c < PARTS))
        def _():
            suffix_chain(c)

        @pl.when(t == gain_step)
        def _():
            gain_second()

        @pl.when(t == gain_step + 2)
        def _():
            gain_third()

        w = t - within_lag

        @pl.when((w >= 0) & (w < PARTS))
        def _():
            for i in range(WIDE):
                within_block(own0 + w * WIDE + i)
                within_block(sib0 + w * WIDE + i)
            for i in range(WIDE):
                store(0, own0 + w * WIDE + i).start()
                store(0, sib0 + w * WIDE + i).start()

        f = t - finish_lag

        @pl.when((f >= 0) & (f < PARTS))
        def _():
            remote(ss.at[part(f)], suf.at[part(f, sib0)], s_sem, f, sib).wait_recv()
            for j in range(WIDE):
                finish(own0 + f * WIDE + j)
                finish(sib0 + f * WIDE + j)
            for j in range(WIDE):
                for i in (1, 2):
                    store(i, own0 + f * WIDE + j).start()
                    store(i, sib0 + f * WIDE + j).start()

    others(n_own, ctx, lambda o: gain_copy(
        gout.at[o], gout.at[o], g3s.at[o], g3r.at[o], {"context": o}).wait_recv())
    for h in range(HEADS):
        sg_ref[:, h * DIM:(h + 1) * DIM] = gout[h // per, h % per]

    last_store = pltpu.make_async_copy(sg_ref, sg_hbm, in_sem.at[0])
    last_store.start()

    @pl.loop(0, HEADS)
    def _(h):
        for i in range(3):
            store(i, h).wait()

    last_store.wait()

    @pl.loop(0, PARTS)
    def _(t):
        swap_local(t).wait_send()
        give_prefix(t).wait_send()
        swap_term(t).wait_send()
        give_suffix(t).wait_send()

        @pl.when(z < last)
        def _():
            pass_prefix(t).wait_send()

        @pl.when(z > 0)
        def _():
            pass_suffix(t).wait_send()

    others(n_own, ctx, lambda o: to_owner(o).wait_send())

    @pl.when(ctx < n_own)
    def _():
        others(n_dp, dp, lambda d: across(d).wait_send())
        others(n_ctx, ctx, lambda c: to_all(c).wait_send())


def write_out(*refs):
    sources, targets, held, sems = refs[:4], refs[4:8], refs[8:12], refs[12]
    cuts = [
        (i, pl.ds(r * 32, 32), r) for r in range(4) for i in range(3)] + [(3, pl.ds(0, 1), 0)]
    ins = [pltpu.make_async_copy(sources[i].at[r], held[i].at[r], sems.at[0, i, n])
           for i, r, n in cuts]
    outs = [pltpu.make_async_copy(held[i].at[r], targets[i].at[r], sems.at[1, i, n])
            for i, r, n in cuts]
    for copy in ins:
        copy.start()
    for load, save in zip(ins, outs):
        load.wait()
        save.start()
    for copy in outs:
        copy.wait()


def shards(n_dp, n_ctx, queries, keys, values, gain, out_grad):
    count, width = queries.shape[1:]
    tokens = queries.shape[0] * n_dp * count * n_ctx
    link_t = BF16 if n_ctx <= 16 else F32
    n_own = min(n_ctx, HEADS)
    per = HEADS // n_own
    flat = lambda x: x.reshape(count, width)
    tile = lambda n, t: pltpu.VMEM((n, DIM, DIM), t)
    hbm = pl.BlockSpec(memory_space=pltpu.HBM)
    dma = pltpu.SemaphoreType.DMA
    outs = pl.pallas_call(
        functools.partial(kernel, n_dp, n_ctx, tokens, link_t),
        out_shape=[jax.ShapeDtypeStruct((count, width), BF16)] * 3
        + [jax.ShapeDtypeStruct((1, width), F32)],
        in_specs=[hbm] * 5,
        out_specs=[hbm] * 4,
        scratch_shapes=[
            *[pltpu.VMEM((count, width), BF16)] * 3,
            pltpu.VMEM((1, width), F32), pltpu.VMEM((count, width), BF16),
            *[pltpu.VMEM((count, width), BF16)] * 3, pltpu.VMEM((1, width), F32),
            tile(HALF, F32), tile(HALF, BF16), tile(HALF, BF16),
            tile(HALF, link_t), tile(HALF, link_t), tile(HALF, BF16), tile(HEADS, BF16),
            tile(HEADS, BF16), tile(HEADS, BF16),
            tile(HALF, F32), tile(HALF, BF16), tile(HALF, BF16),
            tile(HALF, link_t), tile(HALF, link_t), tile(HALF, BF16), tile(HEADS, BF16),
            tile(HEADS, F32), tile(HEADS, F32),
            pltpu.VMEM((HEADS, 1, DIM), F32),
            pltpu.VMEM((n_ctx, per, 1, DIM), F32),
            pltpu.VMEM((n_dp, per, 1, DIM), F32),
            pltpu.VMEM((n_own, per, 1, DIM), F32),
        ]
        + [dma((2, PARTS))] * 6
        + [dma((n_own,)), dma((n_ctx,)), dma((n_dp,)), dma((n_dp,)), dma((n_ctx,)), dma((n_own,)),
           dma((7,)), dma((3, HEADS))],
        compiler_params=pltpu.CompilerParams(
            collective_id=0, has_side_effects=True, vmem_limit_bytes=60 * 2**20),
        cost_estimate=pl.CostEstimate(
            flops=24 * HEADS * DIM**3, bytes_accessed=7 * 2 * count * width,
            transcendentals=HEADS * DIM),
    )(flat(queries), flat(keys), flat(values), gain.reshape(1, width), flat(out_grad))
    outs = pl.pallas_call(
        write_out,
        out_shape=[jax.ShapeDtypeStruct(x.shape, x.dtype) for x in outs],
        in_specs=[hbm] * 4,
        out_specs=[hbm] * 4,
        scratch_shapes=[*[pltpu.VMEM((count, width), BF16)] * 3, pltpu.VMEM((1, width), F32),
                        dma((2, 4, 4))],
        compiler_params=pltpu.CompilerParams(vmem_limit_bytes=60 * 2**20),
    )(*outs)
    shape = (1, count, width)
    return (outs[0].reshape(shape), outs[1].reshape(shape), outs[2].reshape(shape),
            outs[3].reshape(width))


def solution(mesh):
    rows = P("dp", "context", None)
    return jax.shard_map(
        functools.partial(shards, mesh.shape["dp"], mesh.shape["context"]),
        mesh=mesh,
        in_specs=(rows, rows, rows, P(), rows),
        out_specs=(rows, rows, rows, P()),
        check_vma=False,
    )
```

```python
import functools
import math

import jax
import jax.numpy as jnp
from jax import lax
from jax.experimental import pallas as pl
from jax.experimental.pallas import tpu as pltpu
from jax.sharding import PartitionSpec as P

HEADS = 16
HALF = HEADS // 2
DIM = 128
F32 = jnp.float32
BF16 = jnp.bfloat16
MESH = pl.DeviceIdType.MESH


def nn(a, b):
    return lax.dot_general(a, b, (((1,), (0,)), ((), ())), preferred_element_type=F32)


def nt(a, b):
    return lax.dot_general(a, b, (((1,), (1,)), ((), ())), preferred_element_type=F32)


def tn(a, b):
    return lax.dot_general(a, b, (((0,), (0,)), ((), ())), preferred_element_type=F32)


def kernel(
    n_dp, n_ctx, tokens, link_t,
    q_hbm, k_hbm, v_hbm, gain_hbm, dy_hbm,
    qg_hbm, kg_hbm, vg_hbm, sg_hbm,
    q_ref, k_ref, v_ref, dy_ref, gain_ref, qg_ref, kg_ref, vg_ref, sg_ref,
    loc, ps, pr, pre, attn, du, term, rs, rr, suf, kp, vp,
    gloc, g1, g2, gout,
    in_sem, gain_sem, swap_s, swap_r, out_sem, back_s, back_r,
    p_sem, r_sem, g1s, g1r, g2s, g2r, g3s, g3r,
):
    dp = lax.axis_index("dp")
    ctx = lax.axis_index("context")
    chips = n_ctx // 2
    last = chips - 1
    z = ctx // 2
    core = ctx % 2
    sib = z * 2 + (1 - core)
    own0 = core * HALF
    sib0 = (1 - core) * HALF
    per = gout.shape[1]
    n_own = gout.shape[0]
    side = n_own // 2

    def lanes(h):
        return pl.ds(pl.multiple_of(h * DIM, DIM), DIM)

    def half(h):
        return pl.ds(pl.multiple_of(h * DIM, DIM), HALF * DIM)

    pairs = ((k_hbm, k_ref), (v_hbm, v_ref), (q_hbm, q_ref), (dy_hbm, dy_ref))
    loads = [
        pltpu.make_async_copy(src.at[:, half(own0)], dst.at[core], in_sem.at[i])
        for i, (src, dst) in enumerate(pairs)]
    load_gain = pltpu.make_async_copy(gain_hbm.at[:, half(own0)], gain_ref, gain_sem.at[0])
    for load in loads:
        load.start()
    load_gain.start()

    barrier = pltpu.get_barrier_semaphore()

    def others(n, me, f):
        @pl.loop(0, n)
        def _(i):
            @pl.when(i != me)
            def _():
                f(i)

    others(n_ctx, ctx, lambda c: pl.semaphore_signal(
        barrier, inc=1, device_id={"context": c}, device_id_type=MESH))
    others(n_dp, dp, lambda d: pl.semaphore_signal(
        barrier, inc=1, device_id={"dp": d}, device_id_type=MESH))
    pl.semaphore_wait(barrier, n_ctx - 1 + n_dp - 1)

    def copy_to(src, dst, send, recv, device):
        return pltpu.make_async_remote_copy(
            src_ref=src, dst_ref=dst, send_sem=send, recv_sem=recv,
            device_id=device, device_id_type=MESH,
        )

    swaps = [
        copy_to(src.at[:, half(sib0)], dst.at[core], swap_s.at[i], swap_r.at[i], {"context": sib})
        for i, (src, dst) in enumerate(pairs)]
    arrivals = [
        copy_to(src.at[:, half(sib0)], dst.at[1 - core], swap_s.at[i], swap_r.at[i],
                {"context": sib})
        for i, (src, dst) in enumerate(pairs)]
    for swap in swaps:
        swap.start()

    def local_states(b):
        @pl.loop(0, HALF // 4)
        def _(i):
            for j in range(4):
                t = i * 4 + j
                s = lanes(t)
                loc[b, t] = tn(k_ref[b, :, s], v_ref[b, :, s])

    loads[0].wait()
    loads[1].wait()
    local_states(core)

    @pl.when(z == 0)
    def _():
        pr[...] = jnp.zeros_like(pr)

    @pl.when(z == last)
    def _():
        rr[...] = jnp.zeros_like(rr)

    arrivals[0].wait_recv()
    arrivals[1].wait_recv()
    local_states(1 - core)

    def pass_prefix(t):
        return copy_to(ps.at[t], pr.at[t], p_sem.at[0, t], p_sem.at[1, t],
                       {"context": jnp.minimum(ctx + 2, n_ctx - 2 + core)})

    def pass_suffix(t):
        return copy_to(rs.at[t], rr.at[t], r_sem.at[0, t], r_sem.at[1, t],
                       {"context": jnp.maximum(ctx - 2, core)})

    def prefix_chain(t):
        @pl.when(z > 0)
        def _():
            pass_prefix(t).wait_recv()

        before = pr[t].astype(F32)

        @pl.when(z < last)
        def _():
            ps[t] = (before + (loc[0, t] + loc[1, t])).astype(link_t)
            pass_prefix(t).start()

        pre[0, t] = before.astype(BF16)
        pre[1, t] = (before + loc[0, t]).astype(BF16)

    @pl.when(z == 0)
    def _():
        @pl.loop(0, HALF)
        def _(t):
            prefix_chain(t)

    for load in (*loads[2:], load_gain):
        load.wait()
    for arrival in arrivals[2:]:
        arrival.wait_recv()

    rows = lax.broadcasted_iota(jnp.int32, (DIM, DIM), 0)
    cols = lax.broadcasted_iota(jnp.int32, (DIM, DIM), 1)

    @pl.loop(0, HALF // 2)
    def _(i):
        for j in range(2):
            t = i * 2 + j
            s = lanes(t)
            for b in range(2):
                attn[b, t] = jnp.where(
                    rows >= cols, nt(q_ref[b, :, s], k_ref[b, :, s]), 0.0).astype(BF16)

    def norm_step(t):
        s = lanes(t)
        part = []
        for b in range(2):
            u = nn(q_ref[b, :, s], pre[b, t]) + nn(attn[b, t], v_ref[b, :, s])
            inv = lax.rsqrt(jnp.mean(u * u, axis=-1, keepdims=True) + 1e-6)
            unit = u * inv
            grad = dy_ref[b, :, s].astype(F32)
            part.append(jnp.sum(grad * unit, axis=0, keepdims=True))
            scaled = gain_ref[:, s] * grad
            d = (scaled - unit * jnp.mean(scaled * unit, axis=-1, keepdims=True)) * inv
            d = d.astype(BF16)
            du[b, t] = d
            term[b, t] = tn(q_ref[b, :, s], d)
        gloc[t] = part[0] + part[1]

    def suffix_chain(t):
        @pl.when(z < last)
        def _():
            pass_suffix(t).wait_recv()

        after = rr[t].astype(F32)

        @pl.when(z > 0)
        def _():
            rs[t] = (after + (term[0, t] + term[1, t])).astype(link_t)
            pass_suffix(t).start()

        suf[1, t] = after.astype(BF16)
        suf[0, t] = (after + term[1, t]).astype(BF16)

    results = ((qg_ref, qg_hbm), (kg_ref, kg_hbm), (vg_ref, vg_hbm))

    def store(i, t):
        src, dst = results[i]
        return pltpu.make_async_copy(
            src.at[core, :, lanes(t)], dst.at[:, lanes(own0 + t)], out_sem.at[i, t])

    def give_back(i, t, first):
        src, dst = results[i]
        return copy_to(src.at[1 - core, :, lanes(t)], dst.at[:, lanes(first + t)],
                       back_s.at[i, t], back_r.at[i, t], {"context": sib})

    def within_block(t):
        s = lanes(t)
        for b in range(2):
            d = du[b, t]
            da = jnp.where(rows >= cols, nt(d, v_ref[b, :, s]), 0.0).astype(BF16)
            qg_ref[b, :, s] = (nt(d, pre[b, t]) + nn(da, k_ref[b, :, s])).astype(BF16)
            kp[b, t] = tn(da, q_ref[b, :, s])
            vp[b, t] = tn(attn[b, t], d)
        give_back(0, t, own0).start()
        store(0, t).start()

    def finish(t):
        s = lanes(t)
        for b in range(2):
            kg_ref[b, :, s] = (kp[b, t] + nt(v_ref[b, :, s], suf[b, t])).astype(BF16)
            vg_ref[b, :, s] = (vp[b, t] + nn(k_ref[b, :, s], suf[b, t])).astype(BF16)
        for i in (1, 2):
            give_back(i, t, own0).start()
        for i in (1, 2):
            store(i, t).start()

    def to_owner(i):
        return copy_to(gloc.at[pl.ds(i * per, per)], g1.at[z], g1s.at[i], g1r.at[z],
                       {"context": core * side + i})

    def across(d):
        return copy_to(g2.at[dp], g2.at[dp], g2s.at[d], g2r.at[dp], {"dp": d})

    def to_all(c):
        return copy_to(gout.at[ctx], gout.at[ctx], g3s.at[c], g3r.at[ctx], {"context": c})

    mine = ctx - core * side

    def gain_first():
        others(side, mine, lambda i: to_owner(i).start())

        @pl.when((mine >= 0) & (mine < side))
        def _():
            g1[z] = gloc[pl.ds(mine * per, per)]

    def gain_second():
        @pl.when(ctx < n_own)
        def _():
            @pl.loop(0, chips)
            def _(c):
                @pl.when(2 * c + ctx // side != ctx)
                def _():
                    copy_to(gloc.at[pl.ds(0, per)], g1.at[c], g1s.at[0], g1r.at[c],
                            {"context": 2 * c + ctx // side}).wait_recv()

            g2[dp] = jnp.sum(g1[...], axis=0)
            others(n_dp, dp, lambda d: across(d).start())

    def gain_third():
        @pl.when(ctx < n_own)
        def _():
            others(n_dp, dp, lambda d: copy_to(
                g2.at[d], g2.at[d], g2s.at[d], g2r.at[d], {"dp": d}).wait_recv())
            gout[ctx] = jnp.sum(g2[...], axis=0) / jnp.sqrt(F32(tokens))
            others(n_ctx, ctx, lambda c: to_all(c).start())

    chain_lag = jnp.where(
        z == last, 0, jnp.minimum(HALF * (last - z) + 2, 2 * HALF))
    finish_lag = jnp.maximum(chain_lag, HALF)
    gain_step = chain_lag + HALF - 1 - jnp.clip(2 * (last - z - 1), 0, 4)

    @pl.loop(0, 3 * HALF + 3)
    def _(t):
        @pl.when((t < HALF) & (z > 0))
        def _():
            prefix_chain(t)

        @pl.when(t < HALF)
        def _():
            norm_step(t)

        @pl.when(t == HALF - 1)
        def _():
            gain_first()

        c = t - chain_lag

        @pl.when((c >= 0) & (c < HALF))
        def _():
            suffix_chain(c)

        @pl.when(t == gain_step)
        def _():
            gain_second()

        @pl.when(t == gain_step + 2)
        def _():
            gain_third()

        w = t - HALF

        @pl.when((w >= 0) & (w < HALF))
        def _():
            within_block(w)

        f = t - finish_lag

        @pl.when((f >= 0) & (f < HALF))
        def _():
            finish(f)

    others(n_own, ctx, lambda o: copy_to(
        gout.at[o], gout.at[o], g3s.at[o], g3r.at[o], {"context": o}).wait_recv())
    for h in range(HEADS):
        sg_ref[:, h * DIM:(h + 1) * DIM] = gout[h // per, h % per]
    last_store = pltpu.make_async_copy(sg_ref, sg_hbm, gain_sem.at[0])
    last_store.start()

    @pl.loop(0, HALF)
    def _(t):
        for i in range(3):
            store(i, t).wait()
            give_back(i, t, own0).wait_send()
            give_back(i, t, sib0).wait_recv()

        @pl.when(z < last)
        def _():
            pass_prefix(t).wait_send()

        @pl.when(z > 0)
        def _():
            pass_suffix(t).wait_send()

    for swap in swaps:
        swap.wait_send()
    others(side, mine, lambda i: to_owner(i).wait_send())

    @pl.when(ctx < n_own)
    def _():
        others(n_dp, dp, lambda d: across(d).wait_send())
        others(n_ctx, ctx, lambda c: to_all(c).wait_send())

    last_store.wait()


def write_out(*refs):
    sources, targets, held, sems = refs[:4], refs[4:8], refs[8:12], refs[12]
    cuts = [
        (i, pl.ds(r * 32, 32), r) for r in range(4) for i in range(3)] + [(3, pl.ds(0, 1), 0)]
    ins = [pltpu.make_async_copy(sources[i].at[r], held[i].at[r], sems.at[0, i, n])
           for i, r, n in cuts]
    outs = [pltpu.make_async_copy(held[i].at[r], targets[i].at[r], sems.at[1, i, n])
            for i, r, n in cuts]
    for copy in ins:
        copy.start()
    for load, save in zip(ins, outs):
        load.wait()
        save.start()
    for copy in outs:
        copy.wait()


def shards(n_dp, n_ctx, queries, keys, values, gain, out_grad):
    count, width = queries.shape[1:]
    tokens = queries.shape[0] * n_dp * count * n_ctx
    link_t = BF16 if n_ctx <= 16 else F32
    n_own = min(n_ctx, HEADS)
    per = HEADS // n_own
    flat = lambda x: x.reshape(count, width)
    tile = lambda t: pltpu.VMEM((2, HALF, DIM, DIM), t)
    hbm = pl.BlockSpec(memory_space=pltpu.HBM)
    dma = pltpu.SemaphoreType.DMA
    outs = pl.pallas_call(
        functools.partial(kernel, n_dp, n_ctx, tokens, link_t),
        out_shape=[jax.ShapeDtypeStruct((count, width), BF16)] * 3
        + [jax.ShapeDtypeStruct((1, width), F32)],
        in_specs=[hbm] * 5,
        out_specs=[hbm] * 4,
        scratch_shapes=[
            *[pltpu.VMEM((2, count, width // 2), BF16)] * 4, pltpu.VMEM((1, width // 2), F32),
            *[pltpu.VMEM((2, count, width // 2), BF16)] * 3, pltpu.VMEM((1, width), F32),
            tile(F32), pltpu.VMEM((HALF, DIM, DIM), link_t), pltpu.VMEM((HALF, DIM, DIM), link_t),
            tile(BF16), tile(BF16), tile(BF16), tile(F32),
            pltpu.VMEM((HALF, DIM, DIM), link_t), pltpu.VMEM((HALF, DIM, DIM), link_t),
            tile(BF16), tile(F32), tile(F32),
            pltpu.VMEM((HALF, 1, DIM), F32),
            pltpu.VMEM((n_ctx // 2, per, 1, DIM), F32),
            pltpu.VMEM((n_dp, per, 1, DIM), F32),
            pltpu.VMEM((n_own, per, 1, DIM), F32),
            dma((4,)), dma((1,)), dma((4,)), dma((4,)), *[dma((3, HALF))] * 3,
            dma((2, HALF)), dma((2, HALF)), dma((n_own // 2,)), dma((n_ctx // 2,)),
            dma((n_dp,)), dma((n_dp,)), dma((n_ctx,)), dma((n_own,)),
        ],
        compiler_params=pltpu.CompilerParams(
            collective_id=0, has_side_effects=True, vmem_limit_bytes=60 * 2**20),
        cost_estimate=pl.CostEstimate(
            flops=24 * HEADS * DIM**3, bytes_accessed=7 * 2 * count * width,
            transcendentals=HEADS * DIM),
    )(flat(queries), flat(keys), flat(values), gain.reshape(1, width), flat(out_grad))
    outs = pl.pallas_call(
        write_out,
        out_shape=[jax.ShapeDtypeStruct(x.shape, x.dtype) for x in outs],
        in_specs=[hbm] * 4,
        out_specs=[hbm] * 4,
        scratch_shapes=[*[pltpu.VMEM((count, width), BF16)] * 3, pltpu.VMEM((1, width), F32),
                        dma((2, 4, 4))],
        compiler_params=pltpu.CompilerParams(vmem_limit_bytes=60 * 2**20),
    )(*outs)
    shape = (1, count, width)
    return (outs[0].reshape(shape), outs[1].reshape(shape), outs[2].reshape(shape),
            outs[3].reshape(width))


def solution(mesh):
    rows = P("dp", "context", None)
    return jax.shard_map(
        functools.partial(shards, mesh.shape["dp"], mesh.shape["context"]),
        mesh=mesh,
        in_specs=(rows, rows, rows, P(), rows),
        out_specs=(rows, rows, rows, P()),
        check_vma=False,
    )
```
